512 devices in a mesh: dp: 8 (over y, core), row: 8 (over z_lo), col: 8 (over z_hi, x).
Axes of the slice: x: 4, y: 4, z: 16 (z_hi: 2, z_lo: 8; z = z_hi * 8 + z_lo), core: 2. Of those that a mesh axis runs over, the one named last changes fastest.
Arguments:
- queries: bfloat16 [8, 1024, 8192], P('dp', 'row', 'col'), may hold values from -6 to 6
- keys_in: bfloat16 [8, 1024, 8192], P('dp', 'row', 'col'), may hold values from -6 to 6
- values_in: bfloat16 [8, 1024, 8192], P('dp', 'row', 'col'), may hold values from -6 to 6
- out_weight: bfloat16 [8, 8, 128, 6144], P(None, 'row', None, 'col'), may hold values from -0.0625 to 0.0625
- out_grad: bfloat16 [8, 1024, 6144], P('dp', 'row', 'col'), may hold values from -4 to 4
Outputs:
- projected: bfloat16 [8, 1024, 6144], P('dp', 'row', 'col')
- grad_queries: bfloat16 [8, 1024, 8192], P('dp', 'row', 'col')
- grad_keys: bfloat16 [8, 1024, 8192], P('dp', 'row', 'col')
- grad_values: bfloat16 [8, 1024, 8192], P('dp', 'row', 'col')
- grad_weight: bfloat16 [8, 8, 128, 6144], P(None, 'row', None, 'col')
The draws below stay inside these ranges and needn't reach their ends.
All inputs are finite; a program needn't handle non-finite values.
Results may differ from the reference program's by a relative error of at most 0.034.
Values may be sent and summed in bfloat16 or wider, within the bound.
No kernel may reach another device: no remote copies, remote signals or barrier semaphores. Data moves between devices by JAX's collectives and lax.ppermute only.
A program may use at most 64 MiB of HBM per device.

```python
import math
import jax
import jax.numpy as jnp
from jax import lax

D = 6144
HEADS = 64
HEAD_DIM = 128
SEQ_LEN = 1024
SEQS = 8
N_ROW = 8
N_COL = 8


def draw_queries(key, part):
    key = jax.random.fold_in(key, 11)
    return jnp.clip(jax.random.normal(key, (SEQS, SEQ_LEN, HEADS * HEAD_DIM), jnp.float32), -6.0, 6.0).astype(jnp.bfloat16)


def draw_keys_in(key, part):
    key = jax.random.fold_in(key, 23)
    return jnp.clip(jax.random.normal(key, (SEQS, SEQ_LEN, HEADS * HEAD_DIM), jnp.float32), -6.0, 6.0).astype(jnp.bfloat16)


def block_scale(key, shape, cuts, least, largest):
    loudness = 1.0
    for position, shards_of in cuts:
        heights = jax.random.uniform(jax.random.fold_in(jax.random.fold_in(key, 6), position), (shards_of,), jnp.float32, least / len(cuts), largest / len(cuts))
        loudness = loudness * jnp.repeat(jnp.exp(heights), shape[position] // shards_of).reshape((-1,) + (1,) * (len(shape) - 1 - position))
    return loudness


def bell_draw(own_key, dims, scale, most, pieces=(), kind=jnp.bfloat16):
    entries = scale * jax.random.normal(own_key, dims, jnp.float32)
    if pieces:
        entries = entries * block_scale(own_key, dims, pieces, -0.22, 0.18)
    return jnp.clip(entries, -most, most).astype(kind)


def setup_inputs(seed: int = 0) -> dict:
    streams_of = jax.random.split(jax.random.key(seed), 6)
    return {
        "queries": draw_queries(jax.random.fold_in(streams_of[5], 71), 0),
        "keys_in": draw_keys_in(jax.random.fold_in(streams_of[5], 71), 0),
        "values_in": bell_draw(streams_of[2], (SEQS, SEQ_LEN, HEADS * HEAD_DIM), 1.0, 6.0, ((0, 8), (1, 8), (2, 8))),
        "out_weight": bell_draw(streams_of[3], (N_COL, HEADS // N_COL, HEAD_DIM, D), (HEADS * HEAD_DIM) ** -0.5, 0.0625, ((1, 8), (3, 8))),
        "out_grad": bell_draw(streams_of[4], (SEQS, SEQ_LEN, D), 0.25, 4.0, ((0, 8), (1, 8), (2, 8))),
    }


def attend_head(inputs):
    query_rows, key_rows, value_rows, grad_rows = inputs
    score_scale = 1.0 / math.sqrt(HEAD_DIM)
    positions = jnp.arange(SEQ_LEN, dtype=jnp.int32)
    scores = jnp.dot(query_rows, key_rows.T, preferred_element_type=jnp.float32) * score_scale
    causal = positions[None, :] <= positions[:, None]
    scores = jnp.where(causal, scores, jnp.float32(-1e+30))
    row_max = lax.optimization_barrier(jnp.max(scores, axis=-1, keepdims=True))
    expo = jnp.exp(scores - row_max)
    probs = expo / lax.optimization_barrier(jnp.sum(expo, axis=-1, keepdims=True))
    probs16 = probs.astype(jnp.bfloat16)
    head_out = jnp.dot(probs16, value_rows, preferred_element_type=jnp.float32).astype(jnp.bfloat16)
    dprobs = jnp.dot(grad_rows, value_rows.T, preferred_element_type=jnp.float32)
    row_dot = lax.optimization_barrier(jnp.sum(probs * dprobs, axis=-1, keepdims=True))
    dscores = (probs * (dprobs - row_dot)).astype(jnp.bfloat16)
    grad_query = (jnp.dot(dscores, key_rows, preferred_element_type=jnp.float32) * score_scale).astype(jnp.bfloat16)
    grad_key = (jnp.dot(dscores.T, query_rows, preferred_element_type=jnp.float32) * score_scale).astype(jnp.bfloat16)
    grad_value = jnp.dot(probs16.T, grad_rows, preferred_element_type=jnp.float32).astype(jnp.bfloat16)
    return (head_out, grad_query, grad_key, grad_value)

def by_heads(matrix):
    return matrix.reshape(SEQ_LEN, HEADS, HEAD_DIM).transpose(1, 0, 2)

def from_heads(stacked):
    return stacked.transpose(1, 0, 2).reshape(SEQ_LEN, HEADS * HEAD_DIM)

def reference(queries, keys_in, values_in, out_weight, out_grad):
    width_all = HEADS * HEAD_DIM
    weight_matrix = out_weight.reshape(width_all, D)
    weight_groups = out_weight.reshape(N_COL, N_ROW, -1, D)
    col_width = D // N_COL

    def replica(weight_sum, inputs):
        query_seq, key_seq, value_seq, grad_seq = inputs
        running = jnp.zeros((SEQ_LEN, width_all), jnp.float32)
        for column_group in range(N_COL):
            lower = column_group * col_width
            partial_value = jnp.dot(grad_seq[:, lower:lower + col_width], weight_matrix[:, lower:lower + col_width].T, preferred_element_type=jnp.float32)
            running = running + lax.optimization_barrier(partial_value.astype(jnp.bfloat16)).astype(jnp.float32)
        head_grad = running.astype(jnp.bfloat16)
        results = lax.map(attend_head, (by_heads(query_seq), by_heads(key_seq), by_heads(value_seq), by_heads(head_grad)))
        head_out = from_heads(results[0])
        grouped = head_out.reshape(SEQ_LEN, N_COL, N_ROW, -1)
        accum = jnp.zeros((SEQ_LEN, D), jnp.float32)
        for group_index in range(N_ROW):
            partial_value = jnp.dot(grouped[:, :, group_index].reshape(SEQ_LEN, -1), weight_groups[:, group_index].reshape(-1, D), preferred_element_type=jnp.float32)
            accum = accum + lax.optimization_barrier(partial_value.astype(jnp.bfloat16)).astype(jnp.float32)
        projected = accum.astype(jnp.bfloat16)
        weight_sum = weight_sum + jnp.dot(head_out.T, grad_seq, preferred_element_type=jnp.float32)
        return (weight_sum, (projected, from_heads(results[1]), from_heads(results[2]), from_heads(results[3])))
    start_sum = jnp.zeros((width_all, D), jnp.float32)
    weight_sum, outputs = lax.scan(replica, start_sum, (queries, keys_in, values_in, out_grad))
    grad_weight = weight_sum.astype(jnp.bfloat16).reshape(N_COL, HEADS // N_COL, HEAD_DIM, D)
    return (outputs[0], outputs[1], outputs[2], outputs[3], grad_weight)
```

```python
import math

import jax
import jax.numpy as jnp
from jax import lax
from jax.sharding import Mesh, PartitionSpec as P

HEAD_DIM = 128
DP = ("y", "core")
ROW = "row"
COL = ("zhi", "x")
RING = ("zhi", "row")
F32 = jnp.float32
BF16 = jnp.bfloat16


def attention_forward(query, key, value):
    seq_len = query.shape[0]
    scale = 1.0 / math.sqrt(HEAD_DIM)
    scores = lax.dot_general(query, key, (((1,), (1,)), ((), ())), preferred_element_type=F32) * scale
    positions = jnp.arange(seq_len, dtype=jnp.int32)
    causal = positions[None, :] <= positions[:, None]
    scores = jnp.where(causal, scores, F32(-1e30))
    row_max = jnp.max(scores, axis=-1, keepdims=True)
    expo = jnp.exp(scores - row_max)
    probs = expo / jnp.sum(expo, axis=-1, keepdims=True)
    head_out = jnp.dot(probs.astype(BF16), value, preferred_element_type=F32).astype(BF16)
    return head_out, probs


def attention_backward(query, key, value, probs, grad):
    scale = 1.0 / math.sqrt(HEAD_DIM)
    dprobs = lax.dot_general(grad, value, (((1,), (1,)), ((), ())), preferred_element_type=F32)
    row_dot = jnp.sum(probs * dprobs, axis=-1, keepdims=True)
    dscores = (probs * (dprobs - row_dot)).astype(BF16)
    d_query = (jnp.dot(dscores, key, preferred_element_type=F32) * scale).astype(BF16)
    over_rows = (((0,), (0,)), ((), ()))
    d_key = (lax.dot_general(dscores, query, over_rows, preferred_element_type=F32) * scale).astype(BF16)
    d_value = lax.dot_general(probs.astype(BF16), grad, over_rows, preferred_element_type=F32).astype(BF16)
    return d_query, d_key, d_value


def shifts(count):
    return [[(i, (i + d) % count) for i in range(count)] for d in range(1, count)]


def body(queries, keys_in, values_in, out_weight, out_grad):
    tok = queries.shape[1]
    n_row = lax.axis_size("row")
    n_x = lax.axis_size("x")
    n_dp = lax.axis_size("y") * lax.axis_size("core")
    seq_len = tok * n_row
    width = out_grad.shape[2]
    zhi = lax.axis_index("zhi")
    dp = lax.axis_index("y") * lax.axis_size("core") + lax.axis_index("core")
    swap = [(0, 1), (1, 0)]

    with jax.named_scope("grad_gather"):
        grad_all = lax.all_gather(out_grad[0], RING, axis=0, tiled=True).reshape(2, seq_len, width)

    with jax.named_scope("qkv_exchange"):
        by_head = lambda a: a[0].reshape(tok, n_row, HEAD_DIM).transpose(1, 0, 2)
        stacked = jnp.stack([by_head(queries), by_head(keys_in), by_head(values_in)], axis=1)
        heads = lax.all_to_all(stacked, ROW, 0, 0, tiled=True)
        query, key, value = (heads[:, i].reshape(seq_len, HEAD_DIM) for i in range(3))

    with jax.named_scope("weight_swap"):
        w_rows = out_weight.reshape(-1, width)
        half = w_rows.shape[0] // 2
        piece = half // n_dp
        away = lax.dynamic_slice_in_dim(w_rows, (1 - zhi) * half + dp * piece, piece, 0)
        arrived = lax.ppermute(away, "zhi", swap)
        w_other = lax.all_gather(arrived, DP, axis=0, tiled=True)
        w_own = lax.dynamic_slice_in_dim(w_rows, zhi * half, half, 0)
        first = zhi == 0
        w0 = jnp.where(first, w_own, w_other)
        w1 = jnp.where(first, w_other, w_own)

    with jax.named_scope("attend"):
        head_out, probs = attention_forward(query, key, value)

    with jax.named_scope("head_gather"):
        x_index = lax.axis_index("x")
        got = [head_out] + [lax.ppermute(head_out, "x", s) for s in shifts(n_x)]
        ordered = jnp.stack(got)
        heads_x = jnp.concatenate(
            [lax.dynamic_index_in_dim(ordered, (x_index - i) % n_x, 0, keepdims=False) for i in range(n_x)], axis=1
        )

    with jax.named_scope("head_grad"):
        over_n = (((1,), (1,)), ((), ()))
        hg = lax.dot_general(grad_all[0], w0, over_n, preferred_element_type=F32)
        hg = hg + lax.dot_general(grad_all[1], w1, over_n, preferred_element_type=F32)
        hg = hg.astype(BF16).reshape(seq_len, n_x, HEAD_DIM).transpose(1, 0, 2)
        hg = lax.all_to_all(hg, "x", 0, 0, tiled=True)
        grad = jnp.sum(hg.astype(F32), axis=0).astype(BF16)

    with jax.named_scope("project"):
        part0 = jnp.dot(heads_x, w0, preferred_element_type=F32).astype(BF16)
        part1 = jnp.dot(heads_x, w1, preferred_element_type=F32).astype(BF16)
        parts = jnp.concatenate([part0, part1], axis=0)
        projected = lax.psum_scatter(parts, RING, scatter_dimension=0, tiled=True)

    with jax.named_scope("weight_grad"):
        over_t = (((0,), (0,)), ((), ()))
        dw = [
            lax.dot_general(heads_x, grad_all[i], over_t, preferred_element_type=F32).astype(BF16) for i in range(2)
        ]
        dw = jnp.stack([m.reshape(n_dp, piece, width) for m in dw], axis=1)
        dw = lax.all_to_all(dw, DP, 0, 0, tiled=True)
        dw = jnp.sum(dw.astype(F32), axis=0).astype(BF16)
        dw_own = lax.dynamic_index_in_dim(dw, zhi, 0, keepdims=False)
        dw_away = lax.dynamic_index_in_dim(dw, 1 - zhi, 0, keepdims=False)
        dw_back = lax.ppermute(dw_away, "zhi", swap)
        own_rows = lax.all_gather(dw_own, DP, axis=0, tiled=True)
        other_rows = lax.all_gather(dw_back, DP, axis=0, tiled=True)
        grad_weight = jnp.concatenate(
            [jnp.where(first, own_rows, other_rows), jnp.where(first, other_rows, own_rows)], axis=0
        ).reshape(out_weight.shape)

    with jax.named_scope("attend_back"):
        grads = attention_backward(query, key, value, probs, grad)

    with jax.named_scope("qkv_return"):
        back = jnp.stack([g.reshape(n_row, tok, HEAD_DIM) for g in grads], axis=1)
        back = lax.all_to_all(back, ROW, 0, 0, tiled=True)
        outs = [back[:, i].transpose(1, 0, 2).reshape(1, tok, n_row * HEAD_DIM) for i in range(3)]
    return (projected[None], *outs, grad_weight)


def solution(mesh):
    fine = Mesh(mesh.devices.reshape(4, 2, 8, 2, 4), ("y", "core", "row", "zhi", "x"))
    act = P(DP, ROW, COL)
    wgt = P(None, ROW, None, COL)
    return jax.shard_map(
        body,
        mesh=fine,
        in_specs=(act, act, act, wgt, act),
        out_specs=(act, act, act, act, wgt),
        check_vma=False,
    )
```

```python
import math

import jax
import jax.numpy as jnp
from jax import lax
from jax.sharding import Mesh, PartitionSpec as P

HEAD_DIM = 128
DP = ("y", "core")
ROW = "row"
COL = ("zhi", "x")
RING = ("zhi", "row")
F32 = jnp.float32
BF16 = jnp.bfloat16


def attention_forward(query, key, value):
    seq_len = query.shape[0]
    scale = 1.0 / math.sqrt(HEAD_DIM)
    scores = lax.dot_general(query, key, (((1,), (1,)), ((), ())), preferred_element_type=F32) * scale
    positions = jnp.arange(seq_len, dtype=jnp.int32)
    causal = positions[None, :] <= positions[:, None]
    scores = jnp.where(causal, scores, F32(-1e30))
    row_max = jnp.max(scores, axis=-1, keepdims=True)
    expo = jnp.exp(scores - row_max)
    probs = expo / jnp.sum(expo, axis=-1, keepdims=True)
    head_out = jnp.dot(probs.astype(BF16), value, preferred_element_type=F32).astype(BF16)
    return head_out, probs


def attention_backward(query, key, value, probs, grad):
    scale = 1.0 / math.sqrt(HEAD_DIM)
    dprobs = lax.dot_general(grad, value, (((1,), (1,)), ((), ())), preferred_element_type=F32)
    row_dot = jnp.sum(probs * dprobs, axis=-1, keepdims=True)
    dscores = (probs * (dprobs - row_dot)).astype(BF16)
    d_query = (jnp.dot(dscores, key, preferred_element_type=F32) * scale).astype(BF16)
    over_rows = (((0,), (0,)), ((), ()))
    d_key = (lax.dot_general(dscores, query, over_rows, preferred_element_type=F32) * scale).astype(BF16)
    d_value = lax.dot_general(probs.astype(BF16), grad, over_rows, preferred_element_type=F32).astype(BF16)
    return d_query, d_key, d_value


def shifts(count):
    return [[(i, (i + d) % count) for i in range(count)] for d in range(1, count)]


def reduce_scatter_dp(blocks, piece):
    n_y, n_core = lax.axis_size("y"), lax.axis_size("core")
    y, core = lax.axis_index("y"), lax.axis_index("core")
    width = blocks[0].shape[1]
    cut = jnp.stack([b.reshape(n_y, n_core, piece, width) for b in blocks], axis=2)
    mine = lax.dynamic_index_in_dim(cut, core, 1, keepdims=False)
    away = lax.dynamic_index_in_dim(cut, 1 - core, 1, keepdims=False)
    mine = (mine.astype(F32) + lax.ppermute(away, "core", [(0, 1), (1, 0)]).astype(F32)).astype(BF16)
    total = lax.dynamic_index_in_dim(mine, y, 0, keepdims=False).astype(F32)
    for d, pairs in enumerate(shifts(n_y), 1):
        sent = lax.dynamic_index_in_dim(mine, (y + d) % n_y, 0, keepdims=False)
        total = total + lax.ppermute(sent, "y", pairs).astype(F32)
    return total.astype(BF16)


def body(queries, keys_in, values_in, out_weight, out_grad):
    tok = queries.shape[1]
    n_row = lax.axis_size("row")
    n_x = lax.axis_size("x")
    n_dp = lax.axis_size("y") * lax.axis_size("core")
    seq_len = tok * n_row
    width = out_grad.shape[2]
    zhi = lax.axis_index("zhi")
    dp = lax.axis_index("y") * lax.axis_size("core") + lax.axis_index("core")
    swap = [(0, 1), (1, 0)]

    with jax.named_scope("grad_gather"):
        grad_all = lax.all_gather(out_grad[0], RING, axis=0, tiled=True).reshape(2, seq_len, width)

    with jax.named_scope("qkv_exchange"):
        by_head = lambda a: a[0].reshape(tok, n_row, HEAD_DIM).transpose(1, 0, 2)
        stacked = jnp.stack([by_head(queries), by_head(keys_in), by_head(values_in)], axis=1)
        heads = lax.all_to_all(stacked, ROW, 0, 0, tiled=True)
        query, key, value = (heads[:, i].reshape(seq_len, HEAD_DIM) for i in range(3))

    with jax.named_scope("weight_swap"):
        w_rows = out_weight.reshape(-1, width)
        half = w_rows.shape[0] // 2
        piece = half // n_dp
        away = lax.dynamic_slice_in_dim(w_rows, (1 - zhi) * half + dp * piece, piece, 0)
        arrived = lax.ppermute(away, "zhi", swap)
        w_other = lax.all_gather(arrived, DP, axis=0, tiled=True)
        w_own = lax.dynamic_slice_in_dim(w_rows, zhi * half, half, 0)
        first = zhi == 0
        w0 = jnp.where(first, w_own, w_other)
        w1 = jnp.where(first, w_other, w_own)

    with jax.named_scope("attend"):
        head_out, probs = attention_forward(query, key, value)

    with jax.named_scope("head_gather"):
        x_index = lax.axis_index("x")
        got = [head_out] + [lax.ppermute(head_out, "x", s) for s in shifts(n_x)]
        ordered = jnp.stack(got)
        heads_x = jnp.concatenate(
            [lax.dynamic_index_in_dim(ordered, (x_index - i) % n_x, 0, keepdims=False) for i in range(n_x)], axis=1
        )

    with jax.named_scope("project"):
        part0 = jnp.dot(heads_x, w0, preferred_element_type=F32).astype(BF16)
        part1 = jnp.dot(heads_x, w1, preferred_element_type=F32).astype(BF16)
        part0, part1, grad_all = lax.optimization_barrier((part0, part1, grad_all))
        parts = jnp.concatenate([part0, part1], axis=0)
        parts, grad_all = lax.optimization_barrier((parts, grad_all))
        projected = lax.psum_scatter(parts, RING, scatter_dimension=0, tiled=True)

    with jax.named_scope("head_grad"):
        over_n = (((1,), (1,)), ((), ()))
        hg = lax.dot_general(grad_all[0], w0, over_n, preferred_element_type=F32)
        hg = hg + lax.dot_general(grad_all[1], w1, over_n, preferred_element_type=F32)
        hg = hg.astype(BF16).reshape(seq_len, n_x, HEAD_DIM).transpose(1, 0, 2)
        hg = lax.all_to_all(hg, "x", 0, 0, tiled=True)
        grad = jnp.sum(hg.astype(F32), axis=0).astype(BF16)

    with jax.named_scope("weight_grad"):
        over_t = (((0,), (0,)), ((), ()))
        dw = [
            lax.dot_general(heads_x, grad_all[i], over_t, preferred_element_type=F32).astype(BF16) for i in range(2)
        ]
        dw = reduce_scatter_dp(dw, piece)
        dw_own = lax.dynamic_index_in_dim(dw, zhi, 0, keepdims=False)
        dw_away = lax.dynamic_index_in_dim(dw, 1 - zhi, 0, keepdims=False)
        dw_back = lax.ppermute(dw_away, "zhi", swap)
        own_rows = lax.all_gather(dw_own, DP, axis=0, tiled=True)
        other_rows = lax.all_gather(dw_back, DP, axis=0, tiled=True)
        grad_weight = jnp.concatenate(
            [jnp.where(first, own_rows, other_rows), jnp.where(first, other_rows, own_rows)], axis=0
        ).reshape(out_weight.shape)

    with jax.named_scope("attend_back"):
        grads = attention_backward(query, key, value, probs, grad)

    with jax.named_scope("qkv_return"):
        back = jnp.stack([g.reshape(n_row, tok, HEAD_DIM) for g in grads], axis=1)
        back = lax.all_to_all(back, ROW, 0, 0, tiled=True)
        outs = [back[:, i].transpose(1, 0, 2).reshape(1, tok, n_row * HEAD_DIM) for i in range(3)]
    return (projected[None], *outs, grad_weight)


def solution(mesh):
    fine = Mesh(mesh.devices.reshape(4, 2, 8, 2, 4), ("y", "core", "row", "zhi", "x"))
    act = P(DP, ROW, COL)
    wgt = P(None, ROW, None, COL)
    return jax.shard_map(
        body,
        mesh=fine,
        in_specs=(act, act, act, wgt, act),
        out_specs=(act, act, act, act, wgt),
        check_vma=False,
    )
```

```python
import math

import jax
import jax.numpy as jnp
from jax import lax
from jax.sharding import Mesh, PartitionSpec as P

HEAD_DIM = 128
DP = ("y", "core")
ROW = "row"
COL = ("zhi", "x")
RING = ("zhi", "row")
F32 = jnp.float32
BF16 = jnp.bfloat16


def attention_forward(query, key, value):
    seq_len = query.shape[0]
    scale = 1.0 / math.sqrt(HEAD_DIM)
    scores = lax.dot_general(query, key, (((1,), (1,)), ((), ())), preferred_element_type=F32) * scale
    positions = jnp.arange(seq_len, dtype=jnp.int32)
    causal = positions[None, :] <= positions[:, None]
    scores = jnp.where(causal, scores, F32(-1e30))
    row_max = jnp.max(scores, axis=-1, keepdims=True)
    expo = jnp.exp(scores - row_max)
    probs = expo / jnp.sum(expo, axis=-1, keepdims=True)
    head_out = jnp.dot(probs.astype(BF16), value, preferred_element_type=F32).astype(BF16)
    return head_out, probs


def attention_backward(query, key, value, probs, grad):
    scale = 1.0 / math.sqrt(HEAD_DIM)
    dprobs = lax.dot_general(grad, value, (((1,), (1,)), ((), ())), preferred_element_type=F32)
    row_dot = jnp.sum(probs * dprobs, axis=-1, keepdims=True)
    dscores = (probs * (dprobs - row_dot)).astype(BF16)
    d_query = (jnp.dot(dscores, key, preferred_element_type=F32) * scale).astype(BF16)
    over_rows = (((0,), (0,)), ((), ()))
    d_key = (lax.dot_general(dscores, query, over_rows, preferred_element_type=F32) * scale).astype(BF16)
    d_value = lax.dot_general(probs.astype(BF16), grad, over_rows, preferred_element_type=F32).astype(BF16)
    return d_query, d_key, d_value


def shifts(count):
    return [[(i, (i + d) % count) for i in range(count)] for d in range(1, count)]


def ring_pairs(step):
    n_row, n_hi = lax.axis_size("row"), lax.axis_size("zhi")
    spot = lambda z: (z % n_row) * n_hi + (z // n_row) % n_hi
    return [(spot(z), spot(z + step)) for z in range(n_row * n_hi)]


def ring_step(up, down):
    return lax.ppermute(up, ("row", "zhi"), ring_pairs(1)), lax.ppermute(down, ("row", "zhi"), ring_pairs(-1))


def ring_place(blocks):
    count = lax.axis_size("row") * lax.axis_size("zhi")
    rows, width = blocks[0].shape
    z = lax.axis_index("zhi") * lax.axis_size("row") + lax.axis_index("row")
    out = jnp.zeros((count * rows, width), blocks[0].dtype)
    for d, block in blocks.items():
        out = lax.dynamic_update_slice_in_dim(out, block, ((z + d) % count) * rows, 0)
    return out


def reduce_scatter_dp(blocks, piece):
    n_y, n_core = lax.axis_size("y"), lax.axis_size("core")
    y, core = lax.axis_index("y"), lax.axis_index("core")
    width = blocks[0].shape[1]
    cut = jnp.stack([b.reshape(n_y, n_core, piece, width) for b in blocks], axis=2)
    mine = lax.dynamic_index_in_dim(cut, core, 1, keepdims=False)
    away = lax.dynamic_index_in_dim(cut, 1 - core, 1, keepdims=False)
    mine = (mine.astype(F32) + lax.ppermute(away, "core", [(0, 1), (1, 0)]).astype(F32)).astype(BF16)
    total = lax.dynamic_index_in_dim(mine, y, 0, keepdims=False).astype(F32)
    for d, pairs in enumerate(shifts(n_y), 1):
        sent = lax.dynamic_index_in_dim(mine, (y + d) % n_y, 0, keepdims=False)
        total = total + lax.ppermute(sent, "y", pairs).astype(F32)
    return total.astype(BF16)


def body(queries, keys_in, values_in, out_weight, out_grad):
    tok = queries.shape[1]
    n_row = lax.axis_size("row")
    n_x = lax.axis_size("x")
    n_dp = lax.axis_size("y") * lax.axis_size("core")
    seq_len = tok * n_row
    width = out_grad.shape[2]
    zhi = lax.axis_index("zhi")
    dp = lax.axis_index("y") * lax.axis_size("core") + lax.axis_index("core")
    swap = [(0, 1), (1, 0)]

    blocks = {0: out_grad[0]}
    up = down = out_grad[0]
    for d in range(1, 5):
        with jax.named_scope("grad_gather"):
            up, down = ring_step(up, down)
            blocks[-d], blocks[d] = up, down

    with jax.named_scope("qkv_exchange"):
        by_head = lambda a: a[0].reshape(tok, n_row, HEAD_DIM).transpose(1, 0, 2)
        stacked = jnp.stack([by_head(queries), by_head(keys_in), by_head(values_in)], axis=1)
        heads = lax.all_to_all(stacked, ROW, 0, 0, tiled=True)
        heads, up, down = lax.optimization_barrier((heads, up, down))
        query, key, value = (heads[:, i].reshape(seq_len, HEAD_DIM) for i in range(3))

    with jax.named_scope("weight_swap"):
        w_rows = out_weight.reshape(-1, width)
        half = w_rows.shape[0] // 2
        piece = half // n_dp
        away = lax.dynamic_slice_in_dim(w_rows, (1 - zhi) * half + dp * piece, piece, 0)
        arrived = lax.ppermute(away, "zhi", swap)
        w_other = lax.all_gather(arrived, DP, axis=0, tiled=True)
        w_own = lax.dynamic_slice_in_dim(w_rows, zhi * half, half, 0)
        first = zhi == 0
        w0 = jnp.where(first, w_own, w_other)
        w1 = jnp.where(first, w_other, w_own)

    with jax.named_scope("attend"):
        head_out, probs = attention_forward(query, key, value)

    with jax.named_scope("grad_gather"):
        up, down = ring_step(up, down)
        blocks[-5], blocks[5] = up, down
        head_out, up, down = lax.optimization_barrier((head_out, up, down))
        for d in (6, 7):
            up, down = ring_step(up, down)
            blocks[-d], blocks[d] = up, down

    with jax.named_scope("head_gather"):
        x_index = lax.axis_index("x")
        got = [head_out] + [lax.ppermute(head_out, "x", s) for s in shifts(n_x)]
        *got, up, down = lax.optimization_barrier((*got, up, down))
        ordered = jnp.stack(got)
        heads_x = jnp.concatenate(
            [lax.dynamic_index_in_dim(ordered, (x_index - i) % n_x, 0, keepdims=False) for i in range(n_x)], axis=1
        )

    with jax.named_scope("project"):
        part0 = jnp.dot(heads_x, w0, preferred_element_type=F32).astype(BF16)
        part1 = jnp.dot(heads_x, w1, preferred_element_type=F32).astype(BF16)
        parts = jnp.concatenate([part0, part1], axis=0)
        projected = lax.psum_scatter(parts, RING, scatter_dimension=0, tiled=True)

    with jax.named_scope("grad_gather"):
        half = tok // 2
        up, down = ring_step(up[:half], down[half:])
        blocks[8] = jnp.concatenate([up, down], axis=0)
        grad_all = ring_place(blocks).reshape(2, seq_len, width)
        parts, grad_all = lax.optimization_barrier((parts, grad_all))

    with jax.named_scope("head_grad"):
        over_n = (((1,), (1,)), ((), ()))
        hg = lax.dot_general(grad_all[0], w0, over_n, preferred_element_type=F32)
        hg = hg + lax.dot_general(grad_all[1], w1, over_n, preferred_element_type=F32)
        hg = hg.astype(BF16).reshape(seq_len, n_x, HEAD_DIM).transpose(1, 0, 2)
        hg = lax.all_to_all(hg, "x", 0, 0, tiled=True)
        grad = jnp.sum(hg.astype(F32), axis=0).astype(BF16)

    with jax.named_scope("weight_grad"):
        over_t = (((0,), (0,)), ((), ()))
        dw = [
            lax.dot_general(heads_x, grad_all[i], over_t, preferred_element_type=F32).astype(BF16) for i in range(2)
        ]
        dw = reduce_scatter_dp(dw, piece)
        dw_own = lax.dynamic_index_in_dim(dw, zhi, 0, keepdims=False)
        dw_away = lax.dynamic_index_in_dim(dw, 1 - zhi, 0, keepdims=False)
        dw_back = lax.ppermute(dw_away, "zhi", swap)
        own_rows = lax.all_gather(dw_own, DP, axis=0, tiled=True)
        other_rows = lax.all_gather(dw_back, DP, axis=0, tiled=True)
        grad_weight = jnp.concatenate(
            [jnp.where(first, own_rows, other_rows), jnp.where(first, other_rows, own_rows)], axis=0
        ).reshape(out_weight.shape)

    with jax.named_scope("attend_back"):
        grads = attention_backward(query, key, value, probs, grad)

    with jax.named_scope("qkv_return"):
        back = jnp.stack([g.reshape(n_row, tok, HEAD_DIM) for g in grads], axis=1)
        back = lax.all_to_all(back, ROW, 0, 0, tiled=True)
        outs = [back[:, i].transpose(1, 0, 2).reshape(1, tok, n_row * HEAD_DIM) for i in range(3)]
    return (projected[None], *outs, grad_weight)


def solution(mesh):
    fine = Mesh(mesh.devices.reshape(4, 2, 8, 2, 4), ("y", "core", "row", "zhi", "x"))
    act = P(DP, ROW, COL)
    wgt = P(None, ROW, None, COL)
    return jax.shard_map(
        body,
        mesh=fine,
        in_specs=(act, act, act, wgt, act),
        out_specs=(act, act, act, act, wgt),
        check_vma=False,
    )
```

```python
import functools
import math

import jax
import jax.numpy as jnp
from jax import lax
from jax.experimental import pallas as pl
from jax.experimental.pallas import tpu as pltpu
from jax.sharding import Mesh, PartitionSpec as P

HEAD_DIM = 128
DP = ("y", "core")
ROW = "row"
COL = ("zhi", "x")
RING = ("zhi", "row")
F32 = jnp.float32
BF16 = jnp.bfloat16


def attention_forward(query, key, value):
    seq_len = query.shape[0]
    scale = 1.0 / math.sqrt(HEAD_DIM)
    scores = lax.dot_general(query, key, (((1,), (1,)), ((), ())), preferred_element_type=F32) * scale
    positions = jnp.arange(seq_len, dtype=jnp.int32)
    causal = positions[None, :] <= positions[:, None]
    scores = jnp.where(causal, scores, F32(-1e30))
    row_max = jnp.max(scores, axis=-1, keepdims=True)
    expo = jnp.exp(scores - row_max)
    probs = expo / jnp.sum(expo, axis=-1, keepdims=True)
    head_out = jnp.dot(probs.astype(BF16), value, preferred_element_type=F32).astype(BF16)
    return head_out


def backward_kernel(span, n_x, tok, query_ref, key_ref, value_ref, parts_ref, out_ref, key_sum, value_sum):
    seq_len = query_ref.shape[0]
    scale = 1.0 / math.sqrt(HEAD_DIM)
    over_cols = (((1,), (1,)), ((), ()))
    over_rows = (((0,), (0,)), ((), ()))
    key_sum[...] = jnp.zeros_like(key_sum)
    value_sum[...] = jnp.zeros_like(value_sum)
    for first in range(0, seq_len, span):
        past = first + span
        query = query_ref[first:past, :]
        key = key_ref[:past, :]
        value = value_ref[:past, :]
        grad = parts_ref[0, first:past, :].astype(F32)
        for i in range(1, n_x):
            grad = grad + parts_ref[i, first:past, :].astype(F32)
        grad = grad.astype(BF16)
        scores = lax.dot_general(query, key, over_cols, preferred_element_type=F32) * scale
        row = lax.broadcasted_iota(jnp.int32, scores.shape, 0) + first
        col = lax.broadcasted_iota(jnp.int32, scores.shape, 1)
        scores = jnp.where(col <= row, scores, F32(-1e30))
        expo = jnp.exp(scores - jnp.max(scores, axis=-1, keepdims=True))
        probs = expo * (1.0 / jnp.sum(expo, axis=-1, keepdims=True))
        dprobs = lax.dot_general(grad, value, over_cols, preferred_element_type=F32)
        row_dot = jnp.sum(probs * dprobs, axis=-1, keepdims=True)
        dscores = (probs * (dprobs - row_dot)).astype(BF16)
        d_query = (jnp.dot(dscores, key, preferred_element_type=F32) * scale).astype(BF16)
        out_ref[first // tok : past // tok, 0] = d_query.reshape(span // tok, tok, HEAD_DIM)
        key_sum[:past, :] += lax.dot_general(dscores, query, over_rows, preferred_element_type=F32)
        value_sum[:past, :] += lax.dot_general(probs.astype(BF16), grad, over_rows, preferred_element_type=F32)
    blocks = (seq_len // tok, tok, HEAD_DIM)
    out_ref[:, 1] = (key_sum[...] * scale).astype(BF16).reshape(blocks)
    out_ref[:, 2] = value_sum[...].astype(BF16).reshape(blocks)


def attention_backward(query, key, value, parts, tok):
    seq_len = query.shape[0]
    n_x = parts.shape[0]
    span = min(seq_len, 256)
    vmem = pl.BlockSpec(memory_space=pltpu.VMEM)
    return pl.pallas_call(
        functools.partial(backward_kernel, span, n_x, tok),
        out_shape=jax.ShapeDtypeStruct((seq_len // tok, 3, tok, HEAD_DIM), BF16),
        in_specs=[vmem] * 4,
        out_specs=vmem,
        scratch_shapes=[pltpu.VMEM((seq_len, HEAD_DIM), F32)] * 2,
        compiler_params=pltpu.CompilerParams(vmem_limit_bytes=40 * 1024 * 1024),
        cost_estimate=pl.CostEstimate(
            flops=14 * seq_len * seq_len * HEAD_DIM // 2, bytes_accessed=16 * seq_len * HEAD_DIM, transcendentals=seq_len * seq_len // 2
        ),
    )(query, key, value, parts)


def shifts(count):
    return [[(i, (i + d) % count) for i in range(count)] for d in range(1, count)]


def spread_heads(arrays):
    n_row, row = lax.axis_size("row"), lax.axis_index("row")
    tok = arrays[0].shape[0]
    cut = lambda j: jnp.stack([lax.dynamic_slice_in_dim(a, j * HEAD_DIM, HEAD_DIM, 1) for a in arrays])
    out = jnp.zeros((len(arrays), n_row * tok, HEAD_DIM), arrays[0].dtype)
    put = lambda out, part, t: lax.dynamic_update_slice_in_dim(out, part, t * tok, 1)
    got = [lax.ppermute(cut((row + d) % n_row), "row", pairs) for d, pairs in enumerate(shifts(n_row), 1)]
    out = put(out, cut(row), row)
    for d, part in enumerate(got, 1):
        out = put(out, part, (row - d) % n_row)
    return [out[i] for i in range(len(arrays))]


def return_heads(arrays):
    n_row, row = lax.axis_size("row"), lax.axis_index("row")
    tok = arrays[0].shape[0] // n_row
    cut = lambda t: jnp.stack([lax.dynamic_slice_in_dim(a, t * tok, tok, 0) for a in arrays])
    out = jnp.zeros((len(arrays), tok, n_row * HEAD_DIM), arrays[0].dtype)
    put = lambda out, part, j: lax.dynamic_update_slice_in_dim(out, part, j * HEAD_DIM, 2)
    got = [lax.ppermute(cut((row + d) % n_row), "row", pairs) for d, pairs in enumerate(shifts(n_row), 1)]
    out = put(out, cut(row), row)
    for d, part in enumerate(got, 1):
        out = put(out, part, (row - d) % n_row)
    return [out[i] for i in range(len(arrays))]


def reduce_scatter_dp(blocks, piece):
    n_y, n_core = lax.axis_size("y"), lax.axis_size("core")
    y, core = lax.axis_index("y"), lax.axis_index("core")
    width = blocks[0].shape[1]
    cut = jnp.stack([b.reshape(n_y, n_core, piece, width) for b in blocks], axis=2)
    mine = lax.dynamic_index_in_dim(cut, core, 1, keepdims=False)
    away = lax.dynamic_index_in_dim(cut, 1 - core, 1, keepdims=False)
    mine = (mine.astype(F32) + lax.ppermute(away, "core", [(0, 1), (1, 0)]).astype(F32)).astype(BF16)
    total = lax.dynamic_index_in_dim(mine, y, 0, keepdims=False).astype(F32)
    for d, pairs in enumerate(shifts(n_y), 1):
        sent = lax.dynamic_index_in_dim(mine, (y + d) % n_y, 0, keepdims=False)
        total = total + lax.ppermute(sent, "y", pairs).astype(F32)
    return total.astype(BF16)


def body(queries, keys_in, values_in, out_weight, out_grad):
    tok = queries.shape[1]
    n_row = lax.axis_size("row")
    n_x = lax.axis_size("x")
    n_dp = lax.axis_size("y") * lax.axis_size("core")
    seq_len = tok * n_row
    width = out_grad.shape[2]
    zhi = lax.axis_index("zhi")
    dp = lax.axis_index("y") * lax.axis_size("core") + lax.axis_index("core")
    swap = [(0, 1), (1, 0)]

    with jax.named_scope("grad_gather"):
        grad_all = lax.all_gather(out_grad[0], RING, axis=0, tiled=True).reshape(2, seq_len, width)

    with jax.named_scope("qkv_exchange"):
        query, key, value = spread_heads([queries[0], keys_in[0], values_in[0]])

    with jax.named_scope("weight_swap"):
        w_rows = out_weight.reshape(-1, width)
        half = w_rows.shape[0] // 2
        piece = half // n_dp
        away = lax.dynamic_slice_in_dim(w_rows, (1 - zhi) * half + dp * piece, piece, 0)
        arrived = lax.ppermute(away, "zhi", swap)
        w_other = lax.all_gather(arrived, DP, axis=0, tiled=True)
        w_own = lax.dynamic_slice_in_dim(w_rows, zhi * half, half, 0)
        first = zhi == 0
        w0 = jnp.where(first, w_own, w_other)
        w1 = jnp.where(first, w_other, w_own)

    with jax.named_scope("attend"):
        head_out = attention_forward(query, key, value)

    with jax.named_scope("head_gather"):
        x_index = lax.axis_index("x")
        got = [head_out] + [lax.ppermute(head_out, "x", s) for s in shifts(n_x)]
        ordered = jnp.stack(got)
        heads_x = jnp.concatenate(
            [lax.dynamic_index_in_dim(ordered, (x_index - i) % n_x, 0, keepdims=False) for i in range(n_x)], axis=1
        )

    with jax.named_scope("project"):
        part0 = jnp.dot(heads_x, w0, preferred_element_type=F32).astype(BF16)
        part1 = jnp.dot(heads_x, w1, preferred_element_type=F32).astype(BF16)
        parts = jnp.concatenate([part0, part1], axis=0)
        parts, grad_all = lax.optimization_barrier((parts, grad_all))
        projected = lax.psum_scatter(parts, RING, scatter_dimension=0, tiled=True)

    with jax.named_scope("weight_grad"):
        over_t = (((0,), (0,)), ((), ()))
        dw = [
            lax.dot_general(heads_x, grad_all[i], over_t, preferred_element_type=F32).astype(BF16) for i in range(2)
        ]
        *dw, grad_all = lax.optimization_barrier((*dw, grad_all))

    with jax.named_scope("head_grad"):
        over_n = (((1,), (1,)), ((), ()))
        hg = lax.dot_general(grad_all[0], w0, over_n, preferred_element_type=F32)
        hg = hg + lax.dot_general(grad_all[1], w1, over_n, preferred_element_type=F32)
        hg = hg.astype(BF16).reshape(seq_len, n_x, HEAD_DIM).transpose(1, 0, 2)
        grad_parts = lax.all_to_all(hg, "x", 0, 0, tiled=True)

    with jax.named_scope("weight_grad"):
        dw = reduce_scatter_dp(dw, piece)
        dw_own = lax.dynamic_index_in_dim(dw, zhi, 0, keepdims=False)
        dw_away = lax.dynamic_index_in_dim(dw, 1 - zhi, 0, keepdims=False)
        dw_back = lax.ppermute(dw_away, "zhi", swap)
    with jax.named_scope("attend_back"):
        back = attention_backward(query, key, value, grad_parts, tok)

    with jax.named_scope("qkv_return"):
        back, dw_back = lax.optimization_barrier((back, dw_back))
        back = lax.all_to_all(back, ROW, 0, 0, tiled=True)
        outs = [back[:, i].transpose(1, 0, 2).reshape(1, tok, n_row * HEAD_DIM) for i in range(3)]
    with jax.named_scope("weight_grad"):
        own_rows = lax.all_gather(dw_own, DP, axis=0, tiled=True)
        other_rows = lax.all_gather(dw_back, DP, axis=0, tiled=True)
        grad_weight = jnp.concatenate(
            [jnp.where(first, own_rows, other_rows), jnp.where(first, other_rows, own_rows)], axis=0
        ).reshape(out_weight.shape)

    return (projected[None], *outs, grad_weight)


def solution(mesh):
    fine = Mesh(mesh.devices.reshape(4, 2, 8, 2, 4), ("y", "core", "row", "zhi", "x"))
    act = P(DP, ROW, COL)
    wgt = P(None, ROW, None, COL)
    return jax.shard_map(
        body,
        mesh=fine,
        in_specs=(act, act, act, wgt, act),
        out_specs=(act, act, act, act, wgt),
        check_vma=False,
    )
```
